32 devices in a mesh: view: 4 (over y, x), brick: 8 (over z, core).
Axes of the slice: x: 2, y: 2, z: 4, core: 2. Of those that a mesh axis runs over, the one named last changes fastest.
Arguments:
- view_stacks: float32 [4, 128, 256, 256], P('view', 'brick'), may hold values from 0.2 to 5
- point_spread: float32 [4, 128, 256, 256], P('view', 'brick'), may hold values from 0 to 2, as said below
- weights_depth: float32 [4, 128, 128], P('view'), may hold values from 0 to 2, as said below
- weights_rows: float32 [4, 256, 256], P('view'), may hold values from 0 to 2, as said below
- weights_cols: float32 [4, 256, 256], P('view'), may hold values from 0 to 2, as said below
- depth_start: int32 [4, 256, 256], P('view'), may hold values from 0 to 63
- depth_stop: int32 [4, 256, 256], P('view'), may hold values from 65 to 128
Outputs:
- joined_brick: float32 [128, 256, 256], P('brick')
- deconvolved: float32 [128, 256, 256], P('brick')
The draws below stay inside these ranges and needn't reach their ends.
Inputs may be any that keep to these rules, and one draw needn't show every extreme that they name: `point_spread`: nonnegative. `weights_depth`: nonnegative. `weights_rows`: nonnegative. `weights_cols`: nonnegative.
All inputs are finite; a program needn't handle non-finite values.
Results may differ from the reference program's by a relative error of at most 0.00012.
Values sent between devices are 32-bit elements; how exact they have to be, the bound alone decides.
A program may use at most 192 MiB of HBM per device.

```python
import math
import jax
import jax.numpy as jnp
from jax import lax

NZ = 128
NY = 256
NX = 256
VIEWS = 4


def interpolation(key, length):
    first_key, second_key = jax.random.split(key)
    diagonal = jax.random.uniform(first_key, (VIEWS, length, 1), jnp.float32, 0.6, 1.2)
    spread = jax.random.uniform(second_key, (VIEWS, length, length), jnp.float32, 0.0, 1.0)
    spread = spread * (0.6 / length)
    row_index = jnp.arange(length, dtype=jnp.int32)
    identity_mask = (row_index[:, None] == row_index[None, :]).astype(jnp.float32)
    return spread + identity_mask[None] * diagonal


def draw_weights_depth(key, part):
    return interpolation(jax.random.fold_in(key, 11), NZ)


def draw_weights_rows(key, part):
    return interpolation(jax.random.fold_in(key, 12), NY)


def draw_weights_cols(key, part):
    return interpolation(jax.random.fold_in(key, 13), NX)


def circular_offset(length):
    position = jnp.arange(length, dtype=jnp.int32)
    return jnp.minimum(position, length - position).astype(jnp.float32)


def draw_point_spread(key, part):
    split_keys = jax.random.split(jax.random.fold_in(key, 14), 3)
    depth_length = jax.random.uniform(split_keys[0], (VIEWS, 1, 1, 1), jnp.float32, 10.0, 20.0)
    plane_length = jax.random.uniform(split_keys[1], (VIEWS, 1, 1, 1), jnp.float32, 0.5, 1.5)
    roughness = jax.random.uniform(split_keys[2], (VIEWS, NZ, NY, NX), jnp.float32, 0.7, 1.3)
    depth_part = (circular_offset(NZ)[None, :, None, None] / depth_length) ** 2
    row_part = (circular_offset(NY)[None, None, :, None] / plane_length) ** 2
    col_part = (circular_offset(NX)[None, None, None, :] / plane_length) ** 2
    denominator = 1.0 + depth_part + row_part + col_part
    return roughness / (denominator * denominator)


def plant(drawn, key, low, high):
    longest = drawn.shape.index(max(drawn.shape))
    spots = []
    for shift in (0, 1):
        where = [jax.random.randint(jax.random.fold_in(key, axis), (), 0, length) for axis, length in enumerate(drawn.shape)]
        where[longest] = (where[longest] + shift) % drawn.shape[longest]
        spots.append(tuple(where))
    return drawn.at[spots[0]].set(low).at[spots[1]].set(high)


def levels(own_key, shape, shards, smallest, largest):
    loudness, own = 1.0, jax.random.fold_in(own_key, 6)
    for dim, blocks in shards:
        steps = jnp.exp(jax.random.uniform(jax.random.fold_in(own, dim), (blocks,), jnp.float32, smallest / len(shards), largest / len(shards)))
        loudness = loudness * jnp.repeat(steps, shape[dim] // blocks).reshape([-1 if axis == dim else 1 for axis in range(len(shape))])
    return loudness


def setup_inputs(seed: int = 0) -> dict:
    seeds = jax.random.split(jax.random.key(seed), 8)
    view_stacks = jnp.clip(jnp.exp(math.log(5.0) - 3.218876 * jax.random.uniform(seeds[0], (VIEWS, NZ, NY, NX), jnp.float32) ** levels(seeds[0], (VIEWS, NZ, NY, NX), ((0, 4), (1, 8)), -0.2, 0.2)), 0.2, 5.0)
    point_spread = draw_point_spread(jax.random.fold_in(seeds[7], 71), 0)
    weights_depth = draw_weights_depth(jax.random.fold_in(seeds[7], 71), 0)
    weights_rows = draw_weights_rows(jax.random.fold_in(seeds[7], 71), 0)
    weights_cols = draw_weights_cols(jax.random.fold_in(seeds[7], 71), 0)
    depth_start = plant(jax.random.randint(seeds[5], (VIEWS, NY, NX), 0, NZ // 2), jax.random.fold_in(seeds[5], 1), 0, (NZ // 2) - 1).astype(jnp.int32)
    depth_stop = plant(jax.random.randint(seeds[6], (VIEWS, NY, NX), NZ // 2 + 1, NZ + 1), jax.random.fold_in(seeds[6], 1), NZ // 2 + 1, NZ).astype(jnp.int32)
    return dict(view_stacks=view_stacks, point_spread=point_spread, weights_depth=weights_depth, weights_rows=weights_rows, weights_cols=weights_cols, depth_start=depth_start, depth_stop=depth_stop)


def resample_view(source, depth_map, row_map, col_map):
    highest = lax.Precision.HIGHEST
    across = jnp.einsum("zyx,ax->zya", source, col_map, precision=highest)
    across = jnp.einsum("zyx,by->zbx", across, row_map, precision=highest)
    return jnp.einsum("zyx,cz->cyx", across, depth_map, precision=highest)


def reference(view_stacks, point_spread, weights_depth, weights_rows, weights_cols, depth_start, depth_stop):
    depth_grid = jnp.arange(NZ, dtype=jnp.int32)[:, None, None]
    total_signal = jnp.zeros((NZ, NY, NX), jnp.float32)
    total_weight = jnp.zeros((NZ, NY, NX), jnp.float32)
    resampled_list = []
    weight_list = []
    for view_number in range(VIEWS):
        resampled = resample_view(view_stacks[view_number], weights_depth[view_number], weights_rows[view_number], weights_cols[view_number])
        covered = jnp.logical_and(depth_grid >= depth_start[view_number][None], depth_grid < depth_stop[view_number][None]).astype(jnp.float32)
        view_weight = 0.05 + covered * (1.0 + jnp.log(1.0 + resampled * resampled))
        total_signal = total_signal + view_weight * resampled
        total_weight = total_weight + view_weight
        resampled_list.append(resampled)
        weight_list.append(view_weight)
    joined_brick = total_signal / total_weight
    joined_spectrum = jnp.fft.fftn(joined_brick)
    correction_total = jnp.zeros((NZ, NY, NX), jnp.float32)
    for view_number in range(VIEWS):
        transfer = jnp.fft.fftn(point_spread[view_number])
        blurred = jnp.real(jnp.fft.ifftn(joined_spectrum * transfer))
        ratio = resampled_list[view_number] / blurred
        correction = jnp.real(jnp.fft.ifftn(jnp.fft.fftn(ratio) * jnp.conj(transfer)))
        correction_total = correction_total + weight_list[view_number] * correction
    deconvolved = joined_brick * correction_total / total_weight
    return joined_brick, deconvolved
```

```python
import math

import jax
import jax.numpy as jnp
from jax import lax
from jax.sharding import PartitionSpec as P

exact = lax.Precision.HIGH


def dft_tables(rows, columns, length):
    product = rows[:, None] * columns[None, :] % length
    angles = product.astype(jnp.float32) * (2.0 * math.pi / length)
    return jnp.cos(angles), jnp.sin(angles)


def exchange(values):
    return lax.all_to_all(values, "brick", split_axis=0, concat_axis=0)


def dot(form, left, right):
    return jnp.einsum(form, left, right, precision=exact)


def build(mesh):
    blocks, views = mesh.shape["brick"], mesh.shape["view"]

    def per_device(stack, spread, map_depth, map_rows, map_cols, start, stop):
        stack, spread = stack[0], spread[0]
        map_depth, map_rows, map_cols = map_depth[0], map_rows[0], map_cols[0]
        zb, ny, nx = stack.shape
        nz = zb * blocks
        yb = ny // blocks
        yq = yb // views
        half = nx // 2 + 1
        kb = -(-half // blocks)
        kx = kb * blocks

        index = lambda n: jnp.arange(n, dtype=jnp.int32)
        cx, sx = dft_tables(index(kx), index(nx), nx)
        valid = (index(kx) < half)[:, None].astype(jnp.float32)
        into_x = jnp.stack([cx * valid, -sx * valid])
        twice = jnp.where((index(kx) == 0) | (index(kx) == nx // 2), 1.0, 2.0)[:, None] * valid / nx
        from_x = jnp.stack([cx * twice, -sx * twice])
        cz, sz = dft_tables(index(nz), index(nz), nz)
        into_z = jnp.stack([jnp.stack([cz, -sz], 1), jnp.stack([sz, cz], 1)])
        from_z = jnp.stack([jnp.stack([cz, sz], 1), jnp.stack([-sz, cz], 1)]) / nz
        cy, sy = dft_tables(index(ny), index(ny), ny)
        into_z = into_z.reshape(2 * nz, 2 * nz)
        from_z = from_z.reshape(2 * nz, 2 * nz)

        def forward_pencil(values):
            rows = values.shape[0]
            real = dot("kx,yxz->ykz", into_x[0], values)
            imag = dot("kx,yxz->ykz", into_x[1], values)
            both = jnp.concatenate([real, imag], -1)
            both = dot("ykz,zw->kyw", both, into_z)
            return both.reshape(blocks, kb, rows, 2 * nz)

        def backward_pencil(values):
            both = dot("kyz,zw->ykw", values.reshape(kx, yb, 2 * nz), from_z)
            return dot("kx,ykz->yxz", from_x[0], both[..., :nz]) + dot(
                "kx,ykz->yxz", from_x[1], both[..., nz:]
            )

        def forward_rows(values):
            by_cos = dot("wy,kyz->kwz", cy, values)
            by_sin = dot("wy,kyz->kwz", sy, values)
            real = by_cos[..., :nz] + by_sin[..., nz:]
            imag = by_cos[..., nz:] - by_sin[..., :nz]
            return real, imag

        def backward_rows(real, imag):
            values = jnp.concatenate([real, imag], -1)
            by_cos = dot("wy,kyz->kwz", cy / ny, values)
            by_sin = dot("wy,kyz->kwz", sy / ny, values)
            real = by_cos[..., :nz] - by_sin[..., nz:]
            imag = by_cos[..., nz:] + by_sin[..., :nz]
            both = jnp.concatenate([real, imag], -1)
            return both.reshape(kb, blocks, yb, 2 * nz).transpose(1, 0, 2, 3)

        def gather_rows(values):
            return values.transpose(1, 0, 2, 3).reshape(kb, ny, 2 * nz)

        part = dot("zyx,ax->zya", stack, map_cols)
        part = dot("zyx,by->bzx", part, map_rows).reshape(blocks, yb, zb, nx)
        part = exchange(part)
        part = part.transpose(1, 0, 2, 3).reshape(yb, nz, nx)
        resampled = dot("yzx,cz->yxc", part, map_depth)

        first = lax.axis_index("brick") * yb
        depth = index(nz)
        from_depth = lax.dynamic_slice_in_dim(start[0], first, yb, 0)[:, :, None]
        to_depth = lax.dynamic_slice_in_dim(stop[0], first, yb, 0)[:, :, None]
        covered = ((depth >= from_depth) & (depth < to_depth)).astype(jnp.float32)
        view_weight = 0.05 + covered * (1.0 + jnp.log(1.0 + resampled * resampled))
        scatter = lambda values: lax.psum_scatter(
            values, "view", scatter_dimension=0, tiled=True
        )
        signal_part = scatter(view_weight * resampled)
        weight_part = scatter(view_weight)

        real = dot("zyx,kx->kyz", spread, into_x[0])
        imag = dot("zyx,kx->kyz", spread, into_x[1])
        real, imag = (
            dot("wy,kyz->kwz", cy, real) + dot("wy,kyz->kwz", sy, imag),
            dot("wy,kyz->kwz", cy, imag) - dot("wy,kyz->kwz", sy, real),
        )
        both = jnp.stack([real, imag]).reshape(2, blocks, kb, ny, zb)
        both = exchange(both.transpose(1, 2, 0, 4, 3))
        both = both.transpose(1, 2, 0, 3, 4).reshape(kb, 2 * nz, ny)
        otf = dot("kzy,zw->kyw", both, into_z)
        otf_real, otf_imag = otf[..., :nz], otf[..., nz:]

        joined = signal_part / weight_part
        spectrum = exchange(forward_pencil(joined))
        spectrum = lax.all_gather(spectrum, "view", axis=0)
        spectrum = spectrum.transpose(2, 1, 0, 3, 4).reshape(kb, ny, 2 * nz)
        real, imag = forward_rows(spectrum)
        blurred = backward_pencil(
            exchange(
                backward_rows(
                    real * otf_real - imag * otf_imag, real * otf_imag + imag * otf_real
                )
            )
        )
        ratio = resampled / blurred
        real, imag = forward_rows(gather_rows(exchange(forward_pencil(ratio))))
        correction = backward_pencil(
            exchange(
                backward_rows(
                    real * otf_real + imag * otf_imag, imag * otf_real - real * otf_imag
                )
            )
        )
        total = scatter(view_weight * correction)
        deconvolved = joined * total / weight_part

        def to_planes(values):
            values = values.transpose(2, 0, 1).reshape(blocks, zb, yq, nx)
            values = exchange(values)
            values = lax.all_gather(values, "view", axis=0)
            return values.transpose(2, 1, 0, 3, 4).reshape(zb, ny, nx)

        return to_planes(joined), to_planes(deconvolved)

    return per_device


def solution(mesh):
    whole, flat, plane = (
        P("view", "brick", None, None),
        P("view", None, None),
        P("brick", None, None),
    )
    return jax.shard_map(
        build(mesh),
        mesh=mesh,
        in_specs=(whole, whole, flat, flat, flat, flat, flat),
        out_specs=(plane, plane),
        check_vma=False,
    )
```

```python
import functools
import math

import jax
import jax.numpy as jnp
from jax import lax
from jax.experimental import pallas as pl
from jax.experimental.pallas import tpu as pltpu
from jax.sharding import PartitionSpec as P

exact = lax.Precision.HIGH


def dft_tables(rows, columns, length):
    product = rows[:, None] * columns[None, :] % length
    angles = product.astype(jnp.float32) * (2.0 * math.pi / length)
    return jnp.cos(angles), jnp.sin(angles)


def exchange(values):
    return lax.all_to_all(values, "brick", split_axis=0, concat_axis=0)


def dot(form, left, right):
    return jnp.einsum(form, left, right, precision=exact)


def halves(values):
    top = values.astype(jnp.bfloat16)
    return top, (values - top.astype(jnp.float32)).astype(jnp.bfloat16)


def pair_dot(left, right):
    once = lambda a, b: jnp.dot(a, b, preferred_element_type=jnp.float32)
    return once(left[0], right[0]) + (once(left[0], right[1]) + once(left[1], right[0]))


def rows_kernel(sign, values, transfer, forth_hi, forth_lo, back_hi, back_lo, out):
    ny, nz = transfer.shape[1], transfer.shape[2] // 2
    spectrum = pair_dot((forth_hi[...], forth_lo[...]), halves(values[...].reshape(ny, 2 * nz)))
    real = spectrum[:ny, :nz] + spectrum[ny:, nz:]
    imag = spectrum[:ny, nz:] - spectrum[ny:, :nz]
    otf_real, otf_imag = transfer[0, :, :nz], sign * transfer[0, :, nz:]
    product = jnp.concatenate(
        [real * otf_real - imag * otf_imag, real * otf_imag + imag * otf_real], -1
    )
    spectrum = pair_dot((back_hi[...], back_lo[...]), halves(product))
    real = spectrum[:ny, :nz] - spectrum[ny:, nz:]
    imag = spectrum[:ny, nz:] + spectrum[ny:, :nz]
    out[...] = jnp.concatenate([real, imag], -1).reshape(out.shape)


def pencil_back(values, z_table, x_table):
    kx, rows, nz = values.shape[0], values.shape[1], values.shape[2] // 2
    flat = pair_dot(halves(values[...].reshape(kx * rows, 2 * nz)), z_table)
    turned = jnp.swapaxes(flat.reshape(kx, rows, 2 * nz), 0, 1)
    wide = jnp.concatenate(
        [
            jnp.concatenate([turned[row, :, part * nz : (part + 1) * nz] for row in range(rows)], -1)
            for part in range(2)
        ],
        0,
    )
    return pair_dot(x_table, halves(wide))


def pencil_forth(wide, x_table, z_table, out):
    kx, rows, nz = out.shape[0], out.shape[1], out.shape[2] // 2
    lines = pair_dot(x_table, halves(wide))
    turned = jnp.stack(
        [
            jnp.concatenate(
                [lines[part * kx : (part + 1) * kx, row * nz : (row + 1) * nz] for part in range(2)], -1
            )
            for row in range(rows)
        ],
        0,
    )
    flat = jnp.swapaxes(turned, 0, 1).reshape(kx * rows, 2 * nz)
    out[...] = pair_dot(halves(flat), z_table).reshape(kx, rows, 2 * nz)


def widen(values):
    return jnp.concatenate([values[row] for row in range(values.shape[0])], -1)


def ratio_kernel(values, resampled, bz, bzl, bx, bxl, fx, fxl, fz, fzl, out):
    wide = pencil_back(values, (bz[...], bzl[...]), (bx[...], bxl[...]))
    pencil_forth(
        widen(resampled) / wide, (fx[...], fxl[...]), (fz[...], fzl[...]), out
    )


def weigh_kernel(values, weight, bz, bzl, bx, bxl, out):
    rows, nz = weight.shape[0], weight.shape[2]
    wide = pencil_back(values, (bz[...], bzl[...]), (bx[...], bxl[...]))
    for row in range(rows):
        out[row] = weight[row] * wide[:, row * nz : (row + 1) * nz]


def forth_kernel(values, fx, fxl, fz, fzl, out):
    pencil_forth(widen(values), (fx[...], fxl[...]), (fz[...], fzl[...]), out)


def call(kernel, grid, specs, out_shape, out_spec, operands):
    return pl.pallas_call(
        kernel,
        grid=(grid,),
        in_specs=specs,
        out_specs=out_spec,
        out_shape=jax.ShapeDtypeStruct(out_shape, jnp.float32),
        compiler_params=pltpu.CompilerParams(vmem_limit_bytes=48 << 20),
    )(*operands)


def fixed(table):
    return pl.BlockSpec(table.shape, lambda step: (0,) * table.ndim)


def build(mesh):
    blocks, views = mesh.shape["brick"], mesh.shape["view"]

    def per_device(stack, spread, map_depth, map_rows, map_cols, start, stop):
        stack, spread = stack[0], spread[0]
        map_depth, map_rows, map_cols = map_depth[0], map_rows[0], map_cols[0]
        zb, ny, nx = stack.shape
        nz = zb * blocks
        yb = ny // blocks
        yq = yb // views
        half = nx // 2 + 1
        kb = -(-half // blocks)
        kx = kb * blocks

        index = lambda n: jnp.arange(n, dtype=jnp.int32)
        cx, sx = dft_tables(index(kx), index(nx), nx)
        valid = (index(kx) < half)[:, None].astype(jnp.float32)
        into_x = jnp.stack([cx * valid, -sx * valid])
        twice = jnp.where((index(kx) == 0) | (index(kx) == nx // 2), 1.0, 2.0)[:, None] * valid / nx
        from_x = jnp.stack([cx * twice, -sx * twice])
        cz, sz = dft_tables(index(nz), index(nz), nz)
        into_z = jnp.stack([jnp.stack([cz, -sz], 1), jnp.stack([sz, cz], 1)])
        from_z = jnp.stack([jnp.stack([cz, sz], 1), jnp.stack([-sz, cz], 1)]) / nz
        cy, sy = dft_tables(index(ny), index(ny), ny)
        into_z = into_z.reshape(2 * nz, 2 * nz)
        from_z = from_z.reshape(2 * nz, 2 * nz)

        def forward_pencil(values):
            rows = values.shape[0]
            real = dot("kx,yxz->ykz", into_x[0], values)
            imag = dot("kx,yxz->ykz", into_x[1], values)
            both = jnp.concatenate([real, imag], -1)
            both = dot("ykz,zw->kyw", both, into_z)
            return both.reshape(blocks, kb, rows, 2 * nz)

        def backward_pencil(values):
            both = dot("kyz,zw->ykw", values.reshape(kx, yb, 2 * nz), from_z)
            return dot("kx,ykz->yxz", from_x[0], both[..., :nz]) + dot(
                "kx,ykz->yxz", from_x[1], both[..., nz:]
            )

        def forward_rows(values):
            by_cos = dot("wy,kyz->kwz", cy, values)
            by_sin = dot("wy,kyz->kwz", sy, values)
            real = by_cos[..., :nz] + by_sin[..., nz:]
            imag = by_cos[..., nz:] - by_sin[..., :nz]
            return real, imag

        def backward_rows(real, imag):
            values = jnp.concatenate([real, imag], -1)
            by_cos = dot("wy,kyz->kwz", cy / ny, values)
            by_sin = dot("wy,kyz->kwz", sy / ny, values)
            real = by_cos[..., :nz] - by_sin[..., nz:]
            imag = by_cos[..., nz:] + by_sin[..., :nz]
            both = jnp.concatenate([real, imag], -1)
            return both.reshape(kb, blocks, yb, 2 * nz).transpose(1, 0, 2, 3)

        def gather_rows(values):
            return values.transpose(1, 0, 2, 3).reshape(kb, ny, 2 * nz)

        tiled = yb % 8 == 0 and yq % 8 == 0 and kx % 8 == 0 and nz % 128 == 0
        rows = 8
        z_forth, z_back = halves(into_z), halves(from_z)
        x_forth = halves(into_x.reshape(2 * kx, nx))
        x_back = halves(from_x.reshape(2 * kx, nx).T)
        both_y = jnp.concatenate([cy, sy], 0)
        y_forth, y_back = halves(both_y), halves(both_y / ny)
        y_mixed = tuple(
            table.reshape(2 * ny, blocks, views, yq).swapaxes(1, 2).reshape(2 * ny, ny)
            for table in y_forth
        )
        lines_spec = pl.BlockSpec((kx, rows, 2 * nz), lambda step: (0, step, 0))
        cells_spec = pl.BlockSpec((rows, nx, nz), lambda step: (step, 0, 0))

        def forth_lines(values):
            if not tiled:
                return forward_pencil(values)
            tables = x_forth + z_forth
            count = values.shape[0]
            lines = call(
                forth_kernel, count // rows, [cells_spec] + [fixed(t) for t in tables],
                (kx, count, 2 * nz), lines_spec, (values,) + tables,
            )
            return lines.reshape(blocks, kb, count, 2 * nz)

        def ratio_lines(values):
            if not tiled:
                return forward_pencil(resampled / backward_pencil(values))
            tables = z_back + x_back + x_forth + z_forth
            lines = call(
                ratio_kernel, yb // rows,
                [lines_spec, cells_spec] + [fixed(t) for t in tables],
                (kx, yb, 2 * nz), lines_spec,
                (values.reshape(kx, yb, 2 * nz), resampled) + tables,
            )
            return lines.reshape(blocks, kb, yb, 2 * nz)

        def weighed_lines(values):
            if not tiled:
                return view_weight * backward_pencil(values)
            tables = z_back + x_back
            return call(
                weigh_kernel, yb // rows,
                [lines_spec, cells_spec] + [fixed(t) for t in tables],
                (yb, nx, nz), cells_spec,
                (values.reshape(kx, yb, 2 * nz), view_weight) + tables,
            )

        def filter_rows(values, otf, sign, gathered):
            if not tiled:
                if gathered:
                    values = values.transpose(2, 1, 0, 3, 4).reshape(kb, ny, 2 * nz)
                else:
                    values = gather_rows(values)
                real, imag = forward_rows(values)
                otf_real, otf_imag = otf[..., :nz], sign * otf[..., nz:]
                return backward_rows(
                    real * otf_real - imag * otf_imag, real * otf_imag + imag * otf_real
                )
            spec = pl.BlockSpec((blocks, 1, yb, 2 * nz), lambda step: (0, step, 0, 0))
            taken, forth = spec, y_forth
            if gathered:
                taken = pl.BlockSpec(
                    (views, blocks, 1, yq, 2 * nz), lambda step: (0, 0, step, 0, 0)
                )
                forth = y_mixed
            tables = forth + y_back
            return call(
                functools.partial(rows_kernel, sign), kb,
                [taken, pl.BlockSpec((1, ny, 2 * nz), lambda step: (step, 0, 0))]
                + [fixed(t) for t in tables],
                (blocks, kb, yb, 2 * nz), spec, (values, otf) + tables,
            )

        part = dot("zyx,ax->zya", stack, map_cols)
        part = dot("zyx,by->bzx", part, map_rows).reshape(blocks, yb, zb, nx)
        real = dot("zyx,kx->kyz", spread, into_x[0])
        imag = dot("zyx,kx->kyz", spread, into_x[1])
        real, imag = (
            dot("wy,kyz->kwz", cy, real) + dot("wy,kyz->kwz", sy, imag),
            dot("wy,kyz->kwz", cy, imag) - dot("wy,kyz->kwz", sy, real),
        )
        both = jnp.stack([real, imag]).reshape(2, blocks, kb, ny, zb).transpose(1, 2, 0, 4, 3)
        part, both = lax.optimization_barrier((exchange(part), both))
        both = exchange(both)

        part = part.transpose(1, 0, 2, 3).reshape(yb, nz, nx)
        resampled = dot("yzx,cz->yxc", part, map_depth)
        first = lax.axis_index("brick") * yb
        depth = index(nz)
        from_depth = lax.dynamic_slice_in_dim(start[0], first, yb, 0)[:, :, None]
        to_depth = lax.dynamic_slice_in_dim(stop[0], first, yb, 0)[:, :, None]
        covered = ((depth >= from_depth) & (depth < to_depth)).astype(jnp.float32)
        view_weight = 0.05 + covered * (1.0 + jnp.log(1.0 + resampled * resampled))
        scatter = lambda values: lax.psum_scatter(
            values, "view", scatter_dimension=0, tiled=True
        )
        signal_part = scatter(view_weight * resampled)
        weight_part = scatter(view_weight)
        signal_part, weight_part, both = lax.optimization_barrier((signal_part, weight_part, both))

        both = both.transpose(1, 2, 0, 3, 4).reshape(kb, 2 * nz, ny)
        otf = dot("kzy,zw->kyw", both, into_z)

        def by_planes(values):
            return values.transpose(2, 0, 1).reshape(blocks, zb, yq, nx)

        def whole_planes(values):
            values = lax.all_gather(values, "view", axis=0)
            return values.transpose(2, 1, 0, 3, 4).reshape(zb, ny, nx)

        joined = signal_part / weight_part
        spectrum = exchange(forth_lines(joined))
        spectrum, planes = lax.optimization_barrier((spectrum, by_planes(joined)))
        planes = exchange(planes)
        spectrum = lax.all_gather(spectrum, "view", axis=0)
        products, planes = lax.optimization_barrier(
            (filter_rows(spectrum, otf, 1.0, True), planes)
        )
        products, joined_out = lax.optimization_barrier(
            (exchange(products), whole_planes(planes))
        )
        products = exchange(ratio_lines(products))
        products = exchange(filter_rows(products, otf, -1.0, False))
        total = scatter(weighed_lines(products))
        deconvolved = joined * total / weight_part
        return joined_out, whole_planes(exchange(by_planes(deconvolved)))

    return per_device


def solution(mesh):
    whole, flat, plane = (
        P("view", "brick", None, None),
        P("view", None, None),
        P("brick", None, None),
    )
    return jax.shard_map(
        build(mesh),
        mesh=mesh,
        in_specs=(whole, whole, flat, flat, flat, flat, flat),
        out_specs=(plane, plane),
        check_vma=False,
    )
```

```python
import functools
import math

import jax
import jax.numpy as jnp
from jax import lax
from jax.experimental import pallas as pl
from jax.experimental.pallas import tpu as pltpu
from jax.sharding import PartitionSpec as P

exact = lax.Precision.HIGH


def dft_tables(rows, columns, length):
    product = rows[:, None] * columns[None, :] % length
    angles = product.astype(jnp.float32) * (2.0 * math.pi / length)
    return jnp.cos(angles), jnp.sin(angles)


def exchange(values):
    return lax.all_to_all(values, "brick", split_axis=0, concat_axis=0)


def dot(form, left, right):
    return jnp.einsum(form, left, right, precision=exact)


def halves(values):
    top = values.astype(jnp.bfloat16)
    return top, (values - top.astype(jnp.float32)).astype(jnp.bfloat16)


def table_halves(table):
    top = lax.reduce_precision(table, 8, 7)
    return top.astype(jnp.bfloat16), (table - top).astype(jnp.bfloat16)


def pair_dot(left, right):
    once = lambda a, b: jnp.dot(a, b, preferred_element_type=jnp.float32)
    return once(left[0], right[0]) + (once(left[0], right[1]) + once(left[1], right[0]))


def rows_kernel(sign, values, transfer, forth_hi, forth_lo, back_hi, back_lo, *outs):
    ny, nz = transfer.shape[1], transfer.shape[2] // 2
    spectrum = pair_dot((forth_hi[...], forth_lo[...]), halves(values[...].reshape(ny, 2 * nz)))
    real = spectrum[:ny, :nz] + spectrum[ny:, nz:]
    imag = spectrum[:ny, nz:] - spectrum[ny:, :nz]
    otf_real, otf_imag = transfer[0, :, :nz], sign * transfer[0, :, nz:]
    product = jnp.concatenate(
        [real * otf_real - imag * otf_imag, real * otf_imag + imag * otf_real], -1
    )
    spectrum = pair_dot((back_hi[...], back_lo[...]), halves(product))
    real = spectrum[:ny, :nz] - spectrum[ny:, nz:]
    imag = spectrum[:ny, nz:] + spectrum[ny:, :nz]
    lines = jnp.concatenate([real, imag], -1)
    count = ny // len(outs)
    for part, out in enumerate(outs):
        out[...] = lines[part * count : (part + 1) * count].reshape(out.shape)


def pencil_back(values, z_table, x_table):
    kx, rows, nz = values.shape[0], values.shape[1], values.shape[2] // 2
    flat = pair_dot(halves(values[...].reshape(kx * rows, 2 * nz)), z_table)
    turned = jnp.swapaxes(flat.reshape(kx, rows, 2 * nz), 0, 1)
    wide = jnp.concatenate(
        [
            jnp.concatenate([turned[row, :, part * nz : (part + 1) * nz] for row in range(rows)], -1)
            for part in range(2)
        ],
        0,
    )
    return pair_dot(x_table, halves(wide))


def pencil_forth(wide, x_table, z_table, out):
    kx, rows, nz = out.shape[0], out.shape[1], out.shape[2] // 2
    lines = pair_dot(x_table, halves(wide))
    turned = jnp.stack(
        [
            jnp.concatenate(
                [lines[part * kx : (part + 1) * kx, row * nz : (row + 1) * nz] for part in range(2)], -1
            )
            for row in range(rows)
        ],
        0,
    )
    flat = jnp.swapaxes(turned, 0, 1).reshape(kx * rows, 2 * nz)
    out[...] = pair_dot(halves(flat), z_table).reshape(kx, rows, 2 * nz)


def widen(values):
    return jnp.concatenate([values[row] for row in range(values.shape[0])], -1)


def ratio_kernel(values, resampled, bz, bzl, bx, bxl, fx, fxl, fz, fzl, out):
    wide = pencil_back(values, (bz[...], bzl[...]), (bx[...], bxl[...]))
    pencil_forth(
        widen(resampled) / wide, (fx[...], fxl[...]), (fz[...], fzl[...]), out
    )


def weigh_kernel(values, weight, bz, bzl, bx, bxl, out):
    rows, nz = out.shape[0], out.shape[2]
    weight = weight[...].reshape(out.shape)
    wide = pencil_back(values, (bz[...], bzl[...]), (bx[...], bxl[...]))
    for row in range(rows):
        out[row] = weight[row] * wide[:, row * nz : (row + 1) * nz]


def forth_kernel(values, fx, fxl, fz, fzl, out):
    pencil_forth(widen(values), (fx[...], fxl[...]), (fz[...], fzl[...]), out)


def call(kernel, grid, specs, out_shape, out_spec, operands):
    return pl.pallas_call(
        kernel,
        grid=(grid,),
        in_specs=specs,
        out_specs=out_spec,
        out_shape=jax.tree.map(
            lambda shape: jax.ShapeDtypeStruct(shape, jnp.float32),
            out_shape,
            is_leaf=lambda leaf: isinstance(leaf, tuple),
        ),
        compiler_params=pltpu.CompilerParams(vmem_limit_bytes=48 << 20),
    )(*operands)


def fixed(table):
    return pl.BlockSpec(table.shape, lambda step: (0,) * table.ndim)


def build(mesh):
    blocks, views = mesh.shape["brick"], mesh.shape["view"]

    def per_device(stack, spread, map_depth, map_rows, map_cols, start, stop):
        stack, spread = stack[0], spread[0]
        map_depth, map_rows, map_cols = map_depth[0], map_rows[0], map_cols[0]
        zb, ny, nx = stack.shape
        nz = zb * blocks
        yb = ny // blocks
        yq = yb // views
        half = nx // 2 + 1
        kb = -(-half // blocks)
        kx = kb * blocks

        index = lambda n: jnp.arange(n, dtype=jnp.int32)
        cx, sx = dft_tables(index(kx), index(nx), nx)
        valid = (index(kx) < half)[:, None].astype(jnp.float32)
        into_x = jnp.stack([cx * valid, -sx * valid])
        twice = jnp.where((index(kx) == 0) | (index(kx) == nx // 2), 1.0, 2.0)[:, None] * valid / nx
        from_x = jnp.stack([cx * twice, -sx * twice])
        cz, sz = dft_tables(index(nz), index(nz), nz)
        into_z = jnp.stack([jnp.stack([cz, -sz], 1), jnp.stack([sz, cz], 1)])
        from_z = jnp.stack([jnp.stack([cz, sz], 1), jnp.stack([-sz, cz], 1)]) / nz
        cy, sy = dft_tables(index(ny), index(ny), ny)
        into_z = into_z.reshape(2 * nz, 2 * nz)
        from_z = from_z.reshape(2 * nz, 2 * nz)

        def forward_pencil(values):
            rows = values.shape[0]
            real = dot("kx,yxz->ykz", into_x[0], values)
            imag = dot("kx,yxz->ykz", into_x[1], values)
            both = jnp.concatenate([real, imag], -1)
            both = dot("ykz,zw->kyw", both, into_z)
            return both.reshape(blocks, kb, rows, 2 * nz)

        def backward_pencil(values):
            both = dot("kyz,zw->ykw", values.reshape(kx, yb, 2 * nz), from_z)
            return dot("kx,ykz->yxz", from_x[0], both[..., :nz]) + dot(
                "kx,ykz->yxz", from_x[1], both[..., nz:]
            )

        def forward_rows(values):
            by_cos = dot("wy,kyz->kwz", cy, values)
            by_sin = dot("wy,kyz->kwz", sy, values)
            real = by_cos[..., :nz] + by_sin[..., nz:]
            imag = by_cos[..., nz:] - by_sin[..., :nz]
            return real, imag

        def backward_rows(real, imag):
            values = jnp.concatenate([real, imag], -1)
            by_cos = dot("wy,kyz->kwz", cy / ny, values)
            by_sin = dot("wy,kyz->kwz", sy / ny, values)
            real = by_cos[..., :nz] - by_sin[..., nz:]
            imag = by_cos[..., nz:] + by_sin[..., :nz]
            both = jnp.concatenate([real, imag], -1)
            return both.reshape(kb, blocks, yb, 2 * nz).transpose(1, 0, 2, 3)

        def gather_rows(values):
            return values.transpose(1, 0, 2, 3).reshape(kb, ny, 2 * nz)

        tiled = yb % 8 == 0 and yq % 8 == 0 and kx % 8 == 0 and nz % 128 == 0
        rows = 8
        parts = 2 if tiled else 1
        z_forth, z_back = table_halves(into_z), table_halves(from_z)
        x_forth = table_halves(into_x.reshape(2 * kx, nx))
        x_back = table_halves(from_x.reshape(2 * kx, nx).T)
        both_y = jnp.concatenate([cy, sy], 0)
        y_forth, y_back = table_halves(both_y), table_halves(both_y / ny)
        y_mixed = tuple(
            table.reshape(2 * ny, blocks, views, yq).swapaxes(1, 2).reshape(2 * ny, ny)
            for table in y_forth
        )
        y_parted = tuple(
            table.reshape(2, blocks, views, parts, yq // parts, ny)
            .transpose(0, 3, 1, 2, 4, 5)
            .reshape(2 * ny, ny)
            for table in y_back
        )
        lines_spec = pl.BlockSpec((kx, rows, 2 * nz), lambda step: (0, step, 0))
        cells_spec = pl.BlockSpec((rows, nx, nz), lambda step: (step, 0, 0))

        def forth_lines(values):
            if not tiled:
                return forward_pencil(values)
            tables = x_forth + z_forth
            count = values.shape[0]
            lines = call(
                forth_kernel, count // rows, [cells_spec] + [fixed(t) for t in tables],
                (kx, count, 2 * nz), lines_spec, (values,) + tables,
            )
            return lines.reshape(blocks, kb, count, 2 * nz)

        def ratio_lines(values):
            if not tiled:
                return forward_pencil(resampled / backward_pencil(values))
            tables = z_back + x_back + x_forth + z_forth
            lines = call(
                ratio_kernel, yb // rows,
                [lines_spec, cells_spec] + [fixed(t) for t in tables],
                (kx, yb, 2 * nz), lines_spec,
                (values.reshape(kx, yb, 2 * nz), resampled) + tables,
            )
            return lines.reshape(blocks, kb, yb, 2 * nz)

        def weighed_lines(values, part):
            if not tiled:
                return view_weight * backward_pencil(values)
            tables = z_back + x_back
            piece = yq // parts
            group = rows // piece
            weight = view_weight.reshape(views, parts, piece, nx, nz)
            return call(
                weigh_kernel, yb // parts // rows,
                [
                    lines_spec,
                    pl.BlockSpec(
                        (group, 1, piece, nx, nz), lambda step: (step, part, 0, 0, 0)
                    ),
                ]
                + [fixed(t) for t in tables],
                (yb // parts, nx, nz), cells_spec,
                (values.reshape(kx, yb // parts, 2 * nz), weight) + tables,
            )

        def filter_rows(values, otf, sign, gathered):
            if not tiled:
                if gathered:
                    values = values.transpose(2, 1, 0, 3, 4).reshape(kb, ny, 2 * nz)
                else:
                    values = gather_rows(values)
                real, imag = forward_rows(values)
                otf_real, otf_imag = otf[..., :nz], sign * otf[..., nz:]
                return [
                    backward_rows(
                        real * otf_real - imag * otf_imag, real * otf_imag + imag * otf_real
                    )
                ]
            spec = pl.BlockSpec((blocks, 1, yb, 2 * nz), lambda step: (0, step, 0, 0))
            taken, forth, back, count = spec, y_forth, y_parted, parts
            if gathered:
                taken = pl.BlockSpec(
                    (views, blocks, 1, yq, 2 * nz), lambda step: (0, 0, step, 0, 0)
                )
                forth, back, count = y_mixed, y_back, 1
            tables = forth + back
            out_spec = pl.BlockSpec(
                (blocks, 1, yb // count, 2 * nz), lambda step: (0, step, 0, 0)
            )
            return call(
                functools.partial(rows_kernel, sign), kb,
                [taken, pl.BlockSpec((1, ny, 2 * nz), lambda step: (step, 0, 0))]
                + [fixed(t) for t in tables],
                [(blocks, kb, yb // count, 2 * nz)] * count, [out_spec] * count,
                (values, otf) + tables,
            )

        part = dot("zyx,ax->zya", stack, map_cols)
        part = dot("zyx,by->bzx", part, map_rows).reshape(blocks, yb, zb, nx)
        real = dot("zyx,kx->kyz", spread, into_x[0])
        imag = dot("zyx,kx->kyz", spread, into_x[1])
        real, imag = (
            dot("wy,kyz->kwz", cy, real) + dot("wy,kyz->kwz", sy, imag),
            dot("wy,kyz->kwz", cy, imag) - dot("wy,kyz->kwz", sy, real),
        )
        both = jnp.stack([real, imag]).reshape(2, blocks, kb, ny, zb).transpose(1, 2, 0, 4, 3)
        part, both = lax.optimization_barrier((exchange(part), both))
        both = exchange(both)

        part = part.transpose(1, 0, 2, 3).reshape(yb, nz, nx)
        resampled = dot("yzx,cz->yxc", part, map_depth)
        first = lax.axis_index("brick") * yb
        depth = index(nz)
        from_depth = lax.dynamic_slice_in_dim(start[0], first, yb, 0)[:, :, None]
        to_depth = lax.dynamic_slice_in_dim(stop[0], first, yb, 0)[:, :, None]
        covered = ((depth >= from_depth) & (depth < to_depth)).astype(jnp.float32)
        view_weight = 0.05 + covered * (1.0 + jnp.log(1.0 + resampled * resampled))
        scatter = lambda values: lax.psum_scatter(
            values, "view", scatter_dimension=0, tiled=True
        )
        signal_part = scatter(view_weight * resampled)
        weight_part = scatter(view_weight)
        signal_part, weight_part, both = lax.optimization_barrier((signal_part, weight_part, both))

        both = both.transpose(1, 2, 0, 3, 4).reshape(kb, 2 * nz, ny)
        otf = dot("kzy,zw->kyw", both, into_z)

        def by_planes(values):
            values = values.transpose(2, 0, 1).reshape(blocks, zb, values.shape[0], nx)
            return values.swapaxes(1, 2)

        def whole_planes(pieces):
            pieces = [lax.all_gather(piece, "view", axis=0) for piece in pieces]
            values = jnp.stack(pieces)
            return values.transpose(4, 2, 1, 0, 3, 5).reshape(zb, ny, nx)

        joined = signal_part / weight_part
        spectrum = exchange(forth_lines(joined))
        spectrum, planes = lax.optimization_barrier((spectrum, by_planes(joined)))
        planes = exchange(planes)
        spectrum = lax.all_gather(spectrum, "view", axis=0)
        products, planes = lax.optimization_barrier(
            (filter_rows(spectrum, otf, 1.0, True)[0], planes)
        )
        products, joined_out = lax.optimization_barrier(
            (exchange(products), whole_planes([planes]))
        )
        products = exchange(ratio_lines(products))
        pieces = []
        piece = yq // parts
        for part, lines in enumerate(filter_rows(products, otf, -1.0, False)):
            mine = slice(part * piece, (part + 1) * piece)
            total = scatter(weighed_lines(exchange(lines), part))
            if pieces:
                total, pieces[-1] = lax.optimization_barrier((total, pieces[-1]))
            deconvolved = joined[mine] * total / weight_part[mine]
            pieces.append(exchange(by_planes(deconvolved)))
        return joined_out, whole_planes(pieces)

    return per_device


def solution(mesh):
    whole, flat, plane = (
        P("view", "brick", None, None),
        P("view", None, None),
        P("brick", None, None),
    )
    return jax.shard_map(
        build(mesh),
        mesh=mesh,
        in_specs=(whole, whole, flat, flat, flat, flat, flat),
        out_specs=(plane, plane),
        check_vma=False,
    )
```

```python
import functools
import math

import jax
import jax.numpy as jnp
from jax import lax
from jax.experimental import pallas as pl
from jax.experimental.pallas import tpu as pltpu
from jax.sharding import PartitionSpec as P

exact = lax.Precision.HIGH


def dft_tables(rows, columns, length):
    product = rows[:, None] * columns[None, :] % length
    angles = product.astype(jnp.float32) * (2.0 * math.pi / length)
    return jnp.cos(angles), jnp.sin(angles)


def exchange(values):
    return lax.all_to_all(values, "brick", split_axis=0, concat_axis=0)


def dot(form, left, right):
    return jnp.einsum(form, left, right, precision=exact)


def halves(values):
    top = values.astype(jnp.bfloat16)
    return top, (values - top.astype(jnp.float32)).astype(jnp.bfloat16)


def table_halves(table):
    top = lax.reduce_precision(table, 8, 7)
    return top.astype(jnp.bfloat16), (table - top).astype(jnp.bfloat16)


def pair_dot(left, right):
    once = lambda a, b: jnp.dot(a, b, preferred_element_type=jnp.float32)
    return once(left[0], right[0]) + (once(left[0], right[1]) + once(left[1], right[0]))


def rows_kernel(sign, values, transfer, forth_hi, forth_lo, back_hi, back_lo, *outs):
    ny, nz = transfer.shape[1], transfer.shape[2] // 2
    spectrum = pair_dot((forth_hi[...], forth_lo[...]), halves(values[...].reshape(ny, 2 * nz)))
    real = spectrum[:ny, :nz] + spectrum[ny:, nz:]
    imag = spectrum[:ny, nz:] - spectrum[ny:, :nz]
    otf_real, otf_imag = transfer[0, :, :nz], sign * transfer[0, :, nz:]
    product = jnp.concatenate(
        [real * otf_real - imag * otf_imag, real * otf_imag + imag * otf_real], -1
    )
    spectrum = pair_dot((back_hi[...], back_lo[...]), halves(product))
    real = spectrum[:ny, :nz] - spectrum[ny:, nz:]
    imag = spectrum[:ny, nz:] + spectrum[ny:, :nz]
    lines = jnp.concatenate([real, imag], -1)
    count = ny // len(outs)
    for part, out in enumerate(outs):
        out[...] = lines[part * count : (part + 1) * count].reshape(out.shape)


def pencil_back(values, z_table, x_table):
    kx, rows, nz = values.shape[0], values.shape[1], values.shape[2] // 2
    flat = pair_dot(halves(values[...].reshape(kx * rows, 2 * nz)), z_table)
    turned = jnp.swapaxes(flat.reshape(kx, rows, 2 * nz), 0, 1)
    wide = jnp.concatenate(
        [
            jnp.concatenate([turned[row, :, part * nz : (part + 1) * nz] for row in range(rows)], -1)
            for part in range(2)
        ],
        0,
    )
    return pair_dot(x_table, halves(wide))


def pencil_forth(wide, x_table, z_table, out):
    kx, rows, nz = out.shape[0], out.shape[1], out.shape[2] // 2
    lines = pair_dot(x_table, halves(wide))
    turned = jnp.stack(
        [
            jnp.concatenate(
                [lines[part * kx : (part + 1) * kx, row * nz : (row + 1) * nz] for part in range(2)], -1
            )
            for row in range(rows)
        ],
        0,
    )
    flat = jnp.swapaxes(turned, 0, 1).reshape(kx * rows, 2 * nz)
    out[...] = pair_dot(halves(flat), z_table).reshape(kx, rows, 2 * nz)


def widen(values):
    return jnp.concatenate([values[row] for row in range(values.shape[0])], -1)


def ratio_kernel(values, resampled, bz, bzl, bx, bxl, fx, fxl, fz, fzl, out):
    wide = pencil_back(values, (bz[...], bzl[...]), (bx[...], bxl[...]))
    pencil_forth(
        widen(resampled) / wide, (fx[...], fxl[...]), (fz[...], fzl[...]), out
    )


def weigh_kernel(values, weight, bz, bzl, bx, bxl, out):
    rows, nz = out.shape[0], out.shape[2]
    weight = weight[...].reshape(out.shape)
    wide = pencil_back(values, (bz[...], bzl[...]), (bx[...], bxl[...]))
    for row in range(rows):
        out[row] = weight[row] * wide[:, row * nz : (row + 1) * nz]


def forth_kernel(values, fx, fxl, fz, fzl, out):
    pencil_forth(widen(values), (fx[...], fxl[...]), (fz[...], fzl[...]), out)


def call(kernel, grid, specs, out_shape, out_spec, operands):
    return pl.pallas_call(
        kernel,
        grid=(grid,),
        in_specs=specs,
        out_specs=out_spec,
        out_shape=jax.tree.map(
            lambda shape: jax.ShapeDtypeStruct(shape, jnp.float32),
            out_shape,
            is_leaf=lambda leaf: isinstance(leaf, tuple),
        ),
        compiler_params=pltpu.CompilerParams(vmem_limit_bytes=48 << 20),
    )(*operands)


def fixed(table):
    return pl.BlockSpec(table.shape, lambda step: (0,) * table.ndim)


def build(mesh):
    blocks, views = mesh.shape["brick"], mesh.shape["view"]

    def per_device(stack, spread, map_depth, map_rows, map_cols, start, stop):
        stack, spread = stack[0], spread[0]
        map_depth, map_rows, map_cols = map_depth[0], map_rows[0], map_cols[0]
        zb, ny, nx = stack.shape
        nz = zb * blocks
        yb = ny // blocks
        yq = yb // views
        half = nx // 2 + 1
        kb = -(-half // blocks)
        kx = kb * blocks

        index = lambda n: jnp.arange(n, dtype=jnp.int32)
        cx, sx = dft_tables(index(kx), index(nx), nx)
        valid = (index(kx) < half)[:, None].astype(jnp.float32)
        into_x = jnp.stack([cx * valid, -sx * valid])
        twice = jnp.where((index(kx) == 0) | (index(kx) == nx // 2), 1.0, 2.0)[:, None] * valid / nx
        from_x = jnp.stack([cx * twice, -sx * twice])
        cz, sz = dft_tables(index(nz), index(nz), nz)
        into_z = jnp.stack([jnp.stack([cz, -sz], 1), jnp.stack([sz, cz], 1)])
        from_z = jnp.stack([jnp.stack([cz, sz], 1), jnp.stack([-sz, cz], 1)]) / nz
        cy, sy = dft_tables(index(ny), index(ny), ny)
        into_z = into_z.reshape(2 * nz, 2 * nz)
        from_z = from_z.reshape(2 * nz, 2 * nz)

        def forward_pencil(values):
            rows = values.shape[0]
            real = dot("kx,yxz->ykz", into_x[0], values)
            imag = dot("kx,yxz->ykz", into_x[1], values)
            both = jnp.concatenate([real, imag], -1)
            both = dot("ykz,zw->kyw", both, into_z)
            return both.reshape(blocks, kb, rows, 2 * nz)

        def backward_pencil(values):
            both = dot("kyz,zw->ykw", values.reshape(kx, yb, 2 * nz), from_z)
            return dot("kx,ykz->yxz", from_x[0], both[..., :nz]) + dot(
                "kx,ykz->yxz", from_x[1], both[..., nz:]
            )

        def forward_rows(values):
            by_cos = dot("wy,kyz->kwz", cy, values)
            by_sin = dot("wy,kyz->kwz", sy, values)
            real = by_cos[..., :nz] + by_sin[..., nz:]
            imag = by_cos[..., nz:] - by_sin[..., :nz]
            return real, imag

        def backward_rows(real, imag):
            values = jnp.concatenate([real, imag], -1)
            by_cos = dot("wy,kyz->kwz", cy / ny, values)
            by_sin = dot("wy,kyz->kwz", sy / ny, values)
            real = by_cos[..., :nz] - by_sin[..., nz:]
            imag = by_cos[..., nz:] + by_sin[..., :nz]
            both = jnp.concatenate([real, imag], -1)
            return both.reshape(kb, blocks, yb, 2 * nz).transpose(1, 0, 2, 3)

        def gather_rows(values):
            return values.transpose(1, 0, 2, 3).reshape(kb, ny, 2 * nz)

        tiled = yb % 8 == 0 and yq % 8 == 0 and kx % 8 == 0 and nz % 128 == 0
        rows = 8
        parts = 2 if tiled else 1
        z_forth, z_back = table_halves(into_z), table_halves(from_z)
        x_forth = table_halves(into_x.reshape(2 * kx, nx))
        x_back = table_halves(from_x.reshape(2 * kx, nx).T)
        both_y = jnp.concatenate([cy, sy], 0)
        y_forth, y_back = table_halves(both_y), table_halves(both_y / ny)
        y_mixed = tuple(
            table.reshape(2 * ny, blocks, views, yq).swapaxes(1, 2).reshape(2 * ny, ny)
            for table in y_forth
        )
        y_parted = tuple(
            table.reshape(2, blocks, views, parts, yq // parts, ny)
            .transpose(0, 3, 1, 2, 4, 5)
            .reshape(2 * ny, ny)
            for table in y_back
        )
        lines_spec = pl.BlockSpec((kx, rows, 2 * nz), lambda step: (0, step, 0))
        cells_spec = pl.BlockSpec((rows, nx, nz), lambda step: (step, 0, 0))

        def forth_lines(values):
            if not tiled:
                return forward_pencil(values)
            tables = x_forth + z_forth
            count = values.shape[0]
            lines = call(
                forth_kernel, count // rows, [cells_spec] + [fixed(t) for t in tables],
                (kx, count, 2 * nz), lines_spec, (values,) + tables,
            )
            return lines.reshape(blocks, kb, count, 2 * nz)

        def ratio_lines(values):
            if not tiled:
                return forward_pencil(resampled / backward_pencil(values))
            tables = z_back + x_back + x_forth + z_forth
            lines = call(
                ratio_kernel, yb // rows,
                [lines_spec, cells_spec] + [fixed(t) for t in tables],
                (kx, yb, 2 * nz), lines_spec,
                (values.reshape(kx, yb, 2 * nz), resampled) + tables,
            )
            return lines.reshape(blocks, kb, yb, 2 * nz)

        def weighed_lines(values, part):
            if not tiled:
                return view_weight * backward_pencil(values)
            tables = z_back + x_back
            piece = yq // parts
            group = rows // piece
            weight = view_weight.reshape(views, parts, piece, nx, nz)
            return call(
                weigh_kernel, yb // parts // rows,
                [
                    lines_spec,
                    pl.BlockSpec(
                        (group, 1, piece, nx, nz), lambda step: (step, part, 0, 0, 0)
                    ),
                ]
                + [fixed(t) for t in tables],
                (yb // parts, nx, nz), cells_spec,
                (values.reshape(kx, yb // parts, 2 * nz), weight) + tables,
            )

        def filter_rows(values, otf, sign, gathered):
            if not tiled:
                if gathered:
                    values = values.transpose(2, 1, 0, 3, 4).reshape(kb, ny, 2 * nz)
                else:
                    values = gather_rows(values)
                real, imag = forward_rows(values)
                otf_real, otf_imag = otf[..., :nz], sign * otf[..., nz:]
                return [
                    backward_rows(
                        real * otf_real - imag * otf_imag, real * otf_imag + imag * otf_real
                    )
                ]
            spec = pl.BlockSpec((blocks, 1, yb, 2 * nz), lambda step: (0, step, 0, 0))
            taken, forth, back, count = spec, y_forth, y_parted, parts
            if gathered:
                taken = pl.BlockSpec(
                    (views, blocks, 1, yq, 2 * nz), lambda step: (0, 0, step, 0, 0)
                )
                forth, back, count = y_mixed, y_back, 1
            tables = forth + back
            out_spec = pl.BlockSpec(
                (blocks, 1, yb // count, 2 * nz), lambda step: (0, step, 0, 0)
            )
            return call(
                functools.partial(rows_kernel, sign), kb,
                [taken, pl.BlockSpec((1, ny, 2 * nz), lambda step: (step, 0, 0))]
                + [fixed(t) for t in tables],
                [(blocks, kb, yb // count, 2 * nz)] * count, [out_spec] * count,
                (values, otf) + tables,
            )

        part = dot("zyx,ax->zya", stack, map_cols)
        part = dot("zyx,by->bzx", part, map_rows).reshape(blocks, yb, zb, nx)
        real = dot("zyx,kx->kyz", spread, into_x[0])
        imag = dot("zyx,kx->kyz", spread, into_x[1])
        real, imag = (
            dot("wy,kyz->kwz", cy, real) + dot("wy,kyz->kwz", sy, imag),
            dot("wy,kyz->kwz", cy, imag) - dot("wy,kyz->kwz", sy, real),
        )
        both = jnp.stack([real, imag]).reshape(2, blocks, kb, ny, zb).transpose(1, 2, 0, 4, 3)
        part, both = lax.optimization_barrier((exchange(part), both))
        both = exchange(both)

        part = part.transpose(1, 0, 2, 3).reshape(yb, nz, nx)
        resampled = dot("yzx,cz->yxc", part, map_depth)
        first = lax.axis_index("brick") * yb
        depth = index(nz)
        from_depth = lax.dynamic_slice_in_dim(start[0], first, yb, 0)[:, :, None]
        to_depth = lax.dynamic_slice_in_dim(stop[0], first, yb, 0)[:, :, None]
        covered = ((depth >= from_depth) & (depth < to_depth)).astype(jnp.float32)
        view_weight = 0.05 + covered * (1.0 + jnp.log(1.0 + resampled * resampled))
        scatter = lambda values: lax.psum_scatter(
            values, "view", scatter_dimension=0, tiled=True
        )
        signal_part = scatter(view_weight * resampled)
        weight_part = scatter(view_weight)
        signal_part, weight_part, both = lax.optimization_barrier((signal_part, weight_part, both))

        both = both.transpose(1, 2, 0, 3, 4).reshape(kb, 2 * nz, ny)
        otf = dot("kzy,zw->kyw", both, into_z)

        def by_planes(values):
            values = values.transpose(2, 0, 1).reshape(blocks, zb, values.shape[0], nx)
            return values.swapaxes(1, 2)

        def whole_planes(pieces):
            pieces = [lax.all_gather(piece, "view", axis=0) for piece in pieces]
            values = jnp.stack(pieces)
            return values.transpose(4, 2, 1, 0, 3, 5).reshape(zb, ny, nx)

        joined = signal_part / weight_part
        spectrum = exchange(forth_lines(joined))
        spectrum, planes = lax.optimization_barrier((spectrum, by_planes(joined)))
        planes = exchange(planes)
        spectrum = lax.all_gather(spectrum, "view", axis=0)
        products, planes = lax.optimization_barrier(
            (filter_rows(spectrum, otf, 1.0, True)[0], planes)
        )
        products, joined_out = lax.optimization_barrier(
            (exchange(products), whole_planes([planes]))
        )
        products = exchange(ratio_lines(products))
        pieces = []
        piece = yq // parts
        weighed = None
        for part, lines in enumerate(filter_rows(products, otf, -1.0, False)):
            mine = slice(part * piece, (part + 1) * piece)
            if weighed is not None:
                _, lines = lax.optimization_barrier((weighed, lines))
            weighed = weighed_lines(exchange(lines), part)
            total = scatter(weighed)
            if pieces:
                total, pieces[-1] = lax.optimization_barrier((total, pieces[-1]))
            deconvolved = joined[mine] * total / weight_part[mine]
            pieces.append(exchange(by_planes(deconvolved)))
        return joined_out, whole_planes(pieces)

    return per_device


def solution(mesh):
    whole, flat, plane = (
        P("view", "brick", None, None),
        P("view", None, None),
        P("brick", None, None),
    )
    return jax.shard_map(
        build(mesh),
        mesh=mesh,
        in_specs=(whole, whole, flat, flat, flat, flat, flat),
        out_specs=(plane, plane),
        check_vma=False,
    )
```
